256 devices in a mesh: row: 32 (over z, y), col: 8 (over x, core).
Axes of the slice: x: 4, y: 4, z: 8, core: 2. Of those that a mesh axis runs over, the one named last changes fastest.
Arguments:
- tokens: bfloat16 [256, 12288], P('col', 'row'), may hold values from -6 to 6
- grad_out: bfloat16 [256, 12288], P('col', 'row'), may hold values from -1 to 1
- up_weight: bfloat16 [12288, 24576], P('row', 'col'), may hold values from -0.0546875 to 0.0546875
- down_weight: bfloat16 [24576, 12288], P('col', 'row'), may hold values from -0.0390625 to 0.0390625
Outputs:
- grad_in: bfloat16 [256, 12288], P('col', 'row')
- grad_up: bfloat16 [12288, 24576], P('row', 'col')
- grad_down: bfloat16 [24576, 12288], P('col', 'row')
The draws below stay inside these ranges and needn't reach their ends.
All inputs are finite; a program needn't handle non-finite values.
Results may differ from the reference program's by a relative error of at most 0.0049.
Values may be sent and summed in bfloat16 or wider, within the bound.
No kernel may reach another device: no remote copies, remote signals or barrier semaphores. Data moves between devices by JAX's collectives and lax.ppermute only.
A program may use at most 64 MiB of HBM per device.

```python
import jax
import jax.numpy as jnp
from jax import lax

D = 12288
FF = 24576
TOKENS = 256
N_ROW = 32


def shard_levels(key, shape, cuts, low, largest):
    loudness = 1.0
    for position, shards_of in cuts:
        draws = jax.random.uniform(jax.random.fold_in(jax.random.fold_in(key, 6), position), (shards_of,), jnp.float32, low / len(cuts), largest / len(cuts))
        loudness = loudness * jnp.repeat(jnp.exp(draws), shape[position] // shards_of).reshape((-1,) + (1,) * (len(shape) - 1 - position))
    return loudness


def bell_draw(rng, dims, width, limit, cuts=(), kind=jnp.bfloat16):
    loudness = shard_levels(rng, dims, cuts, -0.22, 0.18) if cuts else 1.0
    entries = jax.random.normal(rng, dims, jnp.float32) * width * loudness
    return jnp.minimum(jnp.maximum(entries, -limit), limit).astype(kind)


def setup_inputs(seed: int = 0) -> dict:
    keys = jax.random.split(jax.random.key(seed), 5)
    return {
        "tokens": bell_draw(keys[0], (TOKENS, D), 1.0, 6.0, ((0, 8), (1, 32))),
        "grad_out": bell_draw(keys[1], (TOKENS, D), 0.15, 1.0, ((0, 8), (1, 32))),
        "up_weight": bell_draw(keys[2], (D, FF), D ** -0.5, 0.0546875, ((0, 32), (1, 8))),
        "down_weight": bell_draw(keys[3], (FF, D), FF ** -0.5, 0.0390625, ((0, 8), (1, 32))),
    }


def contract(left, right, left_dim, right_dim):
    return lax.dot_general(left, right, (((left_dim,), (right_dim,)), ((), ())), preferred_element_type=jnp.float32)


def gelu_tanh(values):
    return jax.nn.gelu(values, approximate=True)


def gelu_slope(values):
    return jax.jvp(gelu_tanh, (values,), (jnp.ones_like(values),))[1]


def reference(tokens, grad_out, up_weight, down_weight):
    width_block = D // N_ROW
    tok_blocks = tokens.reshape(TOKENS, N_ROW, width_block).transpose(1, 0, 2)
    grad_blocks = grad_out.reshape(TOKENS, N_ROW, width_block).transpose(1, 0, 2)
    up_blocks = up_weight.reshape(N_ROW, width_block, FF)
    down_blocks = down_weight.reshape(FF, N_ROW, width_block).transpose(1, 0, 2)

    def accumulate(totals, pieces):
        tok_piece, grad_piece, up_piece, down_piece = pieces
        pre_sum = totals[0] + jnp.dot(tok_piece, up_piece, preferred_element_type=jnp.float32)
        back_sum = totals[1] + contract(grad_piece, down_piece, 1, 1)
        return (pre_sum, back_sum), None

    zeros_init = jnp.zeros((TOKENS, FF), jnp.float32)
    sums_out, unused = lax.scan(accumulate, (zeros_init, zeros_init), (tok_blocks, grad_blocks, up_blocks, down_blocks))
    pre_act, grad_hidden = sums_out
    hidden = gelu_tanh(pre_act).astype(jnp.bfloat16)
    grad_pre = (grad_hidden * gelu_slope(pre_act)).astype(jnp.bfloat16)
    grad_down = contract(hidden, grad_out, 0, 0).astype(jnp.bfloat16)
    grad_up = contract(tokens, grad_pre, 0, 0).astype(jnp.bfloat16)
    grad_in = contract(grad_pre, up_weight, 1, 1).astype(jnp.bfloat16)
    return grad_in, grad_up, grad_down
```

```python
import jax
import jax.numpy as jnp
from jax import lax
from jax.sharding import Mesh, PartitionSpec as P

F32, BF16 = jnp.float32, jnp.bfloat16
COL = ("x", "core")
NZ, NY, NC = 8, 4, 8
CHUNKS = 1


def contract(left, right, left_dim, right_dim):
    return lax.dot_general(
        left, right, (((left_dim,), (right_dim,)), ((), ())), preferred_element_type=F32
    )


def gelu_tanh(values):
    return jax.nn.gelu(values, approximate=True)


def gelu_slope(values):
    return jax.jvp(gelu_tanh, (values,), (jnp.ones_like(values),))[1]


def shift_y(value, by):
    return lax.ppermute(value, "y", [(i, (i + by) % NY) for i in range(NY)])


def reduce_y(pre, back):
    rows = pre.shape[0] // NY
    f = [pre[d * rows : (d + 1) * rows] for d in range(NY)]
    g = [back[d * rows : (d + 1) * rows] for d in range(NY)]
    up = shift_y(jnp.concatenate([f[2], g[1]]), 1)
    down = shift_y(jnp.concatenate([g[2], f[3]]), -1)
    up2 = shift_y((f[1].astype(F32) + up[:rows].astype(F32)).astype(BF16), 1)
    down2 = shift_y((g[3].astype(F32) + down[:rows].astype(F32)).astype(BF16), -1)
    pre_sum = f[0].astype(F32) + down[rows:].astype(F32) + up2.astype(F32)
    back_sum = g[0].astype(F32) + up[rows:].astype(F32) + down2.astype(F32)
    return pre_sum, back_sum


def reduce_z(pre, back):
    both = jnp.concatenate([pre, back], axis=1).astype(BF16)
    rows = both.shape[0] // NZ
    parts = lax.all_to_all(both.reshape(NZ, rows, -1), "z", 0, 0)
    total = parts.astype(F32).sum(axis=0)
    return total[:, : pre.shape[1]], total[:, pre.shape[1] :]


def gather_z(value):
    return lax.all_gather(value, "z", axis=0, tiled=True)


def gather_y(hidden, grad):
    rows = hidden.shape[0]
    both = jnp.concatenate([hidden, grad])
    below = shift_y(both, 1)
    above = shift_y(both, -1)
    far_hidden = shift_y(below[:rows], 1)
    far_grad = shift_y(above[rows:], -1)
    return (
        jnp.concatenate([hidden, above[:rows], far_hidden, below[:rows]]),
        jnp.concatenate([grad, above[rows:], far_grad, below[rows:]]),
    )


def shards(tokens, grad_out, up_weight, down_weight):
    width = tokens.shape[1]
    both = lax.all_gather(jnp.concatenate([tokens, grad_out], axis=1), COL, axis=0, tiled=True)
    n_tok = both.shape[0]
    block = n_tok // NY
    start = lax.axis_index("y") * block
    both = lax.dynamic_slice_in_dim(jnp.concatenate([both, both]), start, n_tok, axis=0)
    tok, grad = both[:, :width], both[:, width:]

    hidden_cols = up_weight.shape[1]
    chunk = hidden_cols // CHUNKS
    ups, downs, in_total = [], [], 0.0
    for k in range(CHUNKS):
        up_w = up_weight[:, k * chunk : (k + 1) * chunk]
        down_w = down_weight[k * chunk : (k + 1) * chunk]
        pre = jnp.dot(tok, up_w, preferred_element_type=F32).astype(BF16)
        back = contract(grad, down_w, 1, 1).astype(BF16)
        pre_act, grad_hidden = reduce_z(*reduce_y(pre, back))
        hidden = gelu_tanh(pre_act).astype(BF16)
        grad_pre = (grad_hidden * gelu_slope(pre_act)).astype(BF16)
        gathered = gather_z(jnp.concatenate([hidden, grad_pre], axis=1))
        hidden_all, pre_all = gather_y(gathered[:, :chunk], gathered[:, chunk:])
        in_total = in_total + contract(pre_all, up_w, 1, 1)
        ups.append(contract(tok, pre_all, 0, 0).astype(BF16))
        downs.append(contract(hidden_all, grad, 0, 0).astype(BF16))
    in_total = lax.dynamic_slice_in_dim(
        jnp.concatenate([in_total, in_total]), n_tok - start, n_tok, axis=0
    )
    parts = lax.all_to_all(in_total.reshape(NC, n_tok // NC, width), COL, 0, 0)
    grad_in = parts.sum(axis=0).astype(BF16)
    return grad_in, jnp.concatenate(ups, axis=1), jnp.concatenate(downs, axis=0)


def solution(mesh):
    grid = Mesh(mesh.devices.reshape(NZ, NY, 4, 2), ("z", "y", "x", "core"))
    row = ("z", "y")
    return jax.shard_map(
        shards,
        mesh=grid,
        in_specs=(P(COL, row), P(COL, row), P(row, COL), P(COL, row)),
        out_specs=(P(COL, row), P(row, COL), P(COL, row)),
        check_vma=False,
    )
```

```python
import jax
import jax.numpy as jnp
from jax import lax
from jax.sharding import Mesh, PartitionSpec as P

F32, BF16 = jnp.float32, jnp.bfloat16
COL, ROW = ("x", "core"), ("z", "y")
NZ, NY, NX, NCORE = 8, 4, 4, 2
SIZES = {"z": NZ, "y": NY, "x": NX, "core": NCORE}


def contract(left, right, left_dim, right_dim):
    return lax.dot_general(
        left, right, (((left_dim,), (right_dim,)), ((), ())), preferred_element_type=F32
    )


def gelu_tanh(values):
    return jax.nn.gelu(values, approximate=True)


def gelu_slope(values):
    return jax.jvp(gelu_tanh, (values,), (jnp.ones_like(values),))[1]


def shift(value, axis, by):
    n = SIZES[axis]
    return lax.ppermute(value, axis, [(i, (i + by) % n) for i in range(n)])


def shift_apart(value, axis, by):
    n = SIZES[axis]
    pairs = [
        (i * NCORE + core, (i + by * (1 - 2 * core)) % n * NCORE + core)
        for i in range(n)
        for core in range(NCORE)
    ]
    return lax.ppermute(value, (axis, "core"), pairs)


def swap_cores(value):
    return lax.ppermute(value, "core", [(0, 1), (1, 0)])


def tie(values):
    return lax.optimization_barrier(values)


def roll(value, axis, start):
    n = value.shape[axis]
    return lax.dynamic_slice_in_dim(
        jnp.concatenate([value, value], axis=axis), lax.rem(start + n, n), n, axis=axis
    )


def split_rows(value, n):
    rows = value.shape[0] // n
    return [value[i * rows : (i + 1) * rows] for i in range(n)]


def shards(tokens, grad_out, up_weight, down_weight):
    width = tokens.shape[1]
    z, y, x, core = (lax.axis_index(name) for name in ("z", "y", "x", "core"))
    way = 1 - 2 * core
    n_pair = NZ // 2
    half = n_pair // 2
    unit = tokens.shape[0] // half
    both = jnp.concatenate([tokens, grad_out], axis=1).reshape(half, unit, 2 * width)
    chip = jnp.concatenate([both, swap_cores(both)])
    next_x, far_x, last_x = (shift_apart(chip, "x", -1), shift(chip, "x", 2), shift_apart(chip, "x", 1))
    both = jnp.stack([chip, next_x, far_x, last_x])
    both = roll(roll(both, 0, way * (y - x)), 1, z // 2 - half * core)

    order = (2, 1, 3, 0)
    rows = jnp.concatenate([both[:, j] for j in order], axis=1).reshape(-1, 2 * width)
    pre = split_rows(jnp.dot(rows[:, :width], up_weight, preferred_element_type=F32), NY)
    back = split_rows(contract(rows[:, width:], down_weight, 1, 1), NY)

    def parts_of(first, last):
        at = slice(first * unit, last * unit)
        parts = [jnp.concatenate([p[at], b[at]]) for p, b in zip(pre, back, strict=True)]
        return [parts[0], parts[1], parts[2].astype(BF16), parts[3].astype(BF16)]

    def first_hops(parts):
        return shift_apart(parts[2], "y", 1), shift_apart(parts[3], "y", -1)

    def second_message(parts, relay):
        return (parts[1] + relay.astype(F32)).astype(BF16)

    def finish(parts, message, last):
        return parts[0] + shift_apart(message, "y", 1).astype(F32) + last.astype(F32)

    far, mid, own = parts_of(0, 1), parts_of(1, 3), parts_of(3, 4)
    relay, last_far = first_hops(far)
    message, mid[2], mid[3] = tie((second_message(far, relay), mid[2], mid[3]))
    sum_far = finish(far, message, last_far)
    relay, last_mid = first_hops(mid)
    sum_mid = finish(mid, second_message(mid, relay), last_mid)
    sum_mid, own[2], own[3] = tie((sum_mid.astype(BF16), own[2], own[3]))
    relay, last_own = first_hops(own)
    total = finish(own, second_message(own, relay), last_own)

    total = total + shift(sum_far.astype(BF16), "z", 4).astype(F32)
    pre_1, pre_3, back_1, back_3 = split_rows(sum_mid, 4)
    total = total + shift(jnp.concatenate([pre_1, back_1]), "z", 2).astype(F32)
    total = total + shift(jnp.concatenate([pre_3, back_3]), "z", -2).astype(F32)
    total = total + lax.ppermute(total.astype(BF16), "z", [(i, i ^ 1) for i in range(NZ)]).astype(F32)
    pre_act, grad_hidden = total[:unit], total[unit:]
    hidden = gelu_tanh(pre_act).astype(BF16)
    grad_pre = (grad_hidden * gelu_slope(pre_act)).astype(BF16)

    mine = jnp.concatenate([hidden, grad_pre])
    have_1, have_3 = shift(mine, "z", -2), shift(mine, "z", 2)
    have_2 = shift(mine, "z", 4)

    def neighbours(message):
        return shift_apart(message, "y", -1), shift_apart(message, "y", 1)

    next_own, last_own = neighbours(mine)
    have_1, have_3, next_own, last_own = tie((have_1, have_3, next_own, last_own))
    relay_own = shift_apart(next_own, "y", -1)
    have_mid, have_far = jnp.concatenate([have_1, have_3]), have_2
    next_mid, last_mid = neighbours(have_mid)
    next_far, last_far = neighbours(have_far)
    relay = shift_apart(jnp.concatenate([next_mid, next_far]), "y", -1)

    groups = (
        ((0,), (3, 0, 1, 2), (last_own, mine, next_own, relay_own)),
        ((1, 3), (3, 0, 1), (last_mid, have_mid, next_mid)),
        ((2,), (3, 0, 1), (last_far, have_far, next_far)),
        ((1, 3, 2), (2,), (relay,)),
    )
    in_blocks, up_sum, down_sum = {}, 0.0, 0.0
    for js, es, messages in groups:
        parts = [split_rows(message, 2 * len(js)) for message in messages]
        hidden = jnp.concatenate([row for p in parts for row in p[0::2]])
        grad_pre = jnp.concatenate([row for p in parts for row in p[1::2]])
        rows = jnp.concatenate([both[e, j] for e in es for j in js])
        in_part = contract(grad_pre, up_weight, 1, 1).reshape(len(es), len(js), unit, width)
        for i, j in enumerate(js):
            in_blocks.setdefault(j, []).append(in_part[:, i])
        up_sum = up_sum + contract(rows[:, :width], grad_pre, 0, 0)
        down_sum = down_sum + contract(hidden, rows[:, width:], 0, 0)

    in_total = jnp.stack([jnp.concatenate(in_blocks[j]) for j in range(n_pair)], axis=1)
    in_total = roll(roll(in_total, 0, way * (x - y) + 1), 1, half * core - z // 2)
    other = swap_cores(in_total[:, half:])
    in_chip = [in_total[e, :half] + other[-e % NX] for e in range(NX)]
    in_mine = in_chip[0] + shift(in_chip[2], "x", 2)
    in_mine = in_mine + shift_apart(in_chip[1], "x", 1) + shift_apart(in_chip[3], "x", -1)
    grad_in = in_mine.reshape(half * unit, width).astype(BF16)
    return grad_in, up_sum.astype(BF16), down_sum.astype(BF16)


def solution(mesh):
    grid = Mesh(mesh.devices.reshape(NZ, NY, NX, NCORE), ("z", "y", "x", "core"))
    return jax.shard_map(
        shards,
        mesh=grid,
        in_specs=(P(COL, ROW), P(COL, ROW), P(ROW, COL), P(COL, ROW)),
        out_specs=(P(COL, ROW), P(ROW, COL), P(COL, ROW)),
        check_vma=False,
    )
```

```python
import jax
import jax.numpy as jnp
from jax import lax
from jax.sharding import Mesh, PartitionSpec as P

F32, BF16 = jnp.float32, jnp.bfloat16
COL, ROW = ("x", "core"), ("z", "y")
NZ, NY, NX, NCORE = 8, 4, 4, 2
SIZES = {"z": NZ, "y": NY, "x": NX, "core": NCORE}


def contract(left, right, left_dim, right_dim):
    return lax.dot_general(
        left, right, (((left_dim,), (right_dim,)), ((), ())), preferred_element_type=F32
    )


def gelu_tanh(values):
    return jax.nn.gelu(values, approximate=True)


def gelu_slope(values):
    return jax.jvp(gelu_tanh, (values,), (jnp.ones_like(values),))[1]


def shift(value, axis, by):
    n = SIZES[axis]
    return lax.ppermute(value, axis, [(i, (i + by) % n) for i in range(n)])


def shift_apart(value, axis, by):
    n = SIZES[axis]
    pairs = [
        (i * NCORE + core, (i + by * (1 - 2 * core)) % n * NCORE + core)
        for i in range(n)
        for core in range(NCORE)
    ]
    return lax.ppermute(value, (axis, "core"), pairs)


def shift_between_pairs(value, by):
    return lax.ppermute(value, "z", [(i, (i + by * (2 * (i % 2) - 1)) % NZ) for i in range(NZ)])


def swap_in_pair(value):
    return lax.ppermute(value, "z", [(i, i ^ 1) for i in range(NZ)])


def swap_cores(value):
    return lax.ppermute(value, "core", [(0, 1), (1, 0)])


def tie(values):
    return lax.optimization_barrier(values)


def roll(value, axis, start):
    n = value.shape[axis]
    return lax.dynamic_slice_in_dim(
        jnp.concatenate([value, value], axis=axis), lax.rem(start + n, n), n, axis=axis
    )


def split_rows(value, n):
    rows = value.shape[0] // n
    return [value[i * rows : (i + 1) * rows] for i in range(n)]


def shards(tokens, grad_out, up_weight, down_weight):
    width = tokens.shape[1]
    z, y, x, core = (lax.axis_index(name) for name in ("z", "y", "x", "core"))
    way = 1 - 2 * core
    n_pair = NZ // 2
    half = n_pair // 2
    unit = tokens.shape[0] // half
    both = jnp.concatenate([tokens, grad_out], axis=1).reshape(half, unit, 2 * width)
    chip = jnp.concatenate([both, swap_cores(both)])
    next_x, far_x, last_x = (shift_apart(chip, "x", -1), shift(chip, "x", 2), shift_apart(chip, "x", 1))
    both = jnp.stack([chip, next_x, far_x, last_x])
    pair, odd = z // 2, z % 2 == 1
    both = roll(both, 0, way * (y - x))
    both = roll(
        jnp.where(odd, both, both[:, ::-1]),
        1,
        jnp.where(odd, pair - half * core, half * core + n_pair - 1 - pair),
    )

    order = (2, 1, 3, 0)
    rows = jnp.concatenate([both[:, j] for j in order], axis=1).reshape(-1, 2 * width)
    pre = split_rows(jnp.dot(rows[:, :width], up_weight, preferred_element_type=F32), NY)
    back = split_rows(contract(rows[:, width:], down_weight, 1, 1), NY)

    def parts_of(first, last):
        at = slice(first * unit, last * unit)
        parts = [jnp.concatenate([p[at], b[at]]) for p, b in zip(pre, back, strict=True)]
        return [parts[0], parts[1], parts[2].astype(BF16), parts[3].astype(BF16)]

    def first_hops(parts):
        return shift_apart(parts[2], "y", 1), shift_apart(parts[3], "y", -1)

    def second_message(parts, relay):
        return (parts[1] + relay.astype(F32)).astype(BF16)

    def finish(parts, message, last):
        return parts[0] + shift_apart(message, "y", 1).astype(F32) + last.astype(F32)

    far, mid, own = parts_of(0, 1), parts_of(1, 3), parts_of(3, 4)
    relay, last_far = first_hops(far)
    message, mid[2], mid[3] = tie((second_message(far, relay), mid[2], mid[3]))
    sum_far = finish(far, message, last_far).astype(BF16)
    relay, last_mid = first_hops(mid)
    message = second_message(mid, relay)
    sum_mid = finish(mid, message, last_mid).astype(BF16)
    sum_mid, own[2], own[3] = tie((sum_mid, own[2], own[3]))

    pre_1, pre_3, back_1, back_3 = split_rows(sum_mid, 4)
    from_z = shift_between_pairs(jnp.concatenate([pre_3, back_3]), -2).astype(F32)
    from_z = from_z + shift_between_pairs(jnp.concatenate([pre_1, back_1]), 1).astype(F32)
    from_z = tie(from_z + shift_between_pairs(sum_far, 3).astype(F32))
    relay, last_own = first_hops(own)
    total = finish(own, second_message(own, relay), last_own)
    total = total + from_z
    total = total + swap_in_pair(total.astype(BF16)).astype(F32)
    pre_act, grad_hidden = total[:unit], total[unit:]
    hidden = gelu_tanh(pre_act).astype(BF16)
    grad_pre = (grad_hidden * gelu_slope(pre_act)).astype(BF16)

    def neighbours(message):
        return shift_apart(message, "y", -1), shift_apart(message, "y", 1)

    mine = jnp.concatenate([hidden, grad_pre])
    have_1 = shift_between_pairs(mine, 1)
    have_3 = swap_in_pair(have_1)
    have_2 = shift_between_pairs(have_3, 1)
    have_near = jnp.concatenate([mine, have_1])
    next_near, last_near = neighbours(have_near)
    next_near, have_2, have_3 = tie((next_near, have_2, have_3))
    relay_near = shift_apart(next_near, "y", -1)
    have_far = jnp.concatenate([have_3, have_2])
    next_far, last_far = neighbours(have_far)
    relay_near, relay_far = tie((relay_near, shift_apart(next_far, "y", -1)))

    stages = (
        (((0, 1), (3, 0, 1), (last_near, have_near, next_near)),),
        (
            ((0, 1), (2,), (relay_near,)),
            ((3, 2), (3, 0, 1), (last_far, have_far, next_far)),
            ((3, 2), (2,), (relay_far,)),
        ),
    )
    in_blocks, sums = {}, (0.0, 0.0)
    for stage in stages:
        hidden, grad_pre, rows = [], [], []
        for js, es, messages in stage:
            parts = [split_rows(message, 2 * len(js)) for message in messages]
            hidden += [row for p in parts for row in p[0::2]]
            grad_pre += [row for p in parts for row in p[1::2]]
            rows += [both[e, j] for e in es for j in js]
        hidden, grad_pre, rows = (jnp.concatenate(v) for v in (hidden, grad_pre, rows))
        in_part = iter(split_rows(contract(grad_pre, up_weight, 1, 1), rows.shape[0] // unit))
        for js, es, _ in stage:
            for _ in es:
                for j in js:
                    in_blocks.setdefault(j, []).append(next(in_part))
        sums = tie(sums)
        sums = (
            sums[0] + contract(rows[:, :width], grad_pre, 0, 0),
            sums[1] + contract(hidden, rows[:, width:], 0, 0),
        )
    up_sum, down_sum = sums

    in_total = jnp.stack([jnp.stack(in_blocks[j]) for j in range(n_pair)], axis=1)
    in_total = roll(in_total, 0, way * (x - y) + 1)
    in_total = roll(
        jnp.where(odd, in_total, in_total[:, ::-1]),
        1,
        jnp.where(odd, half * core - pair, half * core + n_pair - 1 - pair),
    )
    other = swap_cores(in_total[:, half:])
    in_chip = [in_total[e, :half] + other[-e % NX] for e in range(NX)]
    in_mine = in_chip[0] + shift(in_chip[2], "x", 2)
    in_mine = in_mine + shift_apart(in_chip[1], "x", 1) + shift_apart(in_chip[3], "x", -1)
    grad_in = in_mine.reshape(half * unit, width).astype(BF16)
    return grad_in, up_sum.astype(BF16), down_sum.astype(BF16)


def solution(mesh):
    grid = Mesh(mesh.devices.reshape(NZ, NY, NX, NCORE), ("z", "y", "x", "core"))
    return jax.shard_map(
        shards,
        mesh=grid,
        in_specs=(P(COL, ROW), P(COL, ROW), P(ROW, COL), P(COL, ROW)),
        out_specs=(P(COL, ROW), P(ROW, COL), P(COL, ROW)),
        check_vma=False,
    )
```

```python
import jax
import jax.numpy as jnp
from jax import lax
from jax.sharding import Mesh, PartitionSpec as P

F32, BF16 = jnp.float32, jnp.bfloat16
COL, ROW = ("x", "core"), ("z", "y")
NZ, NY, NX, NCORE = 8, 4, 4, 2
SIZES = {"z": NZ, "y": NY, "x": NX, "core": NCORE}


def contract(left, right, left_dim, right_dim):
    return lax.dot_general(
        left, right, (((left_dim,), (right_dim,)), ((), ())), preferred_element_type=F32
    )


def gelu_tanh(values):
    return jax.nn.gelu(values, approximate=True)


def gelu_slope(values):
    return jax.jvp(gelu_tanh, (values,), (jnp.ones_like(values),))[1]


def shift(value, axis, by):
    n = SIZES[axis]
    return lax.ppermute(value, axis, [(i, (i + by) % n) for i in range(n)])


def shift_apart(value, axis, by):
    n = SIZES[axis]
    pairs = [
        (i * NCORE + core, (i + by * (1 - 2 * core)) % n * NCORE + core)
        for i in range(n)
        for core in range(NCORE)
    ]
    return lax.ppermute(value, (axis, "core"), pairs)


def shift_between_pairs(value, by):
    return lax.ppermute(value, "z", [(i, (i + by * (2 * (i % 2) - 1)) % NZ) for i in range(NZ)])


def swap_in_pair(value):
    return lax.ppermute(value, "z", [(i, i ^ 1) for i in range(NZ)])


def swap_cores(value):
    return lax.ppermute(value, "core", [(0, 1), (1, 0)])


def tie(values):
    return lax.optimization_barrier(values)


def roll(value, axis, start):
    n = value.shape[axis]
    return lax.dynamic_slice_in_dim(
        jnp.concatenate([value, value], axis=axis), lax.rem(start + n, n), n, axis=axis
    )


def split_rows(value, n):
    rows = value.shape[0] // n
    return [value[i * rows : (i + 1) * rows] for i in range(n)]


def shards(tokens, grad_out, up_weight, down_weight):
    width = tokens.shape[1]
    z, y, x, core = (lax.axis_index(name) for name in ("z", "y", "x", "core"))
    way = 1 - 2 * core
    n_pair = NZ // 2
    half = n_pair // 2
    unit = tokens.shape[0] // half
    both = jnp.concatenate([tokens, grad_out], axis=1).reshape(half, unit, 2 * width)
    chip = jnp.concatenate([both, swap_cores(both)])
    next_x, far_x, last_x = (shift_apart(chip, "x", -1), shift(chip, "x", 2), shift_apart(chip, "x", 1))
    both = jnp.stack([chip, next_x, far_x, last_x])
    pair, odd = z // 2, z % 2 == 1
    both = roll(both, 0, way * (y - x))
    both = roll(
        jnp.where(odd, both, both[:, ::-1]),
        1,
        jnp.where(odd, pair - half * core, half * core + n_pair - 1 - pair),
    )

    order = (2, 1, 3, 0)
    rows = jnp.concatenate([both[:, j] for j in order], axis=1).reshape(-1, 2 * width)
    pre = split_rows(jnp.dot(rows[:, :width], up_weight, preferred_element_type=F32), NY)
    back = split_rows(contract(rows[:, width:], down_weight, 1, 1), NY)

    def parts_of(first, last):
        at = slice(first * unit, last * unit)
        parts = [jnp.concatenate([p[at], b[at]]) for p, b in zip(pre, back, strict=True)]
        return [parts[0], parts[1], parts[2].astype(BF16), parts[3].astype(BF16)]

    def first_hops(parts):
        return shift_apart(parts[2], "y", 1), shift_apart(parts[3], "y", -1)

    def second_message(parts, relay):
        return (parts[1] + relay.astype(F32)).astype(BF16)

    def finish(parts, message, last):
        return parts[0] + shift_apart(message, "y", 1).astype(F32) + last.astype(F32)

    far, mid, own = parts_of(0, 1), parts_of(1, 3), parts_of(3, 4)
    relay, last_far = first_hops(far)
    message, mid[2], mid[3] = tie((second_message(far, relay), mid[2], mid[3]))
    sum_far = finish(far, message, last_far).astype(BF16)
    relay, last_mid = first_hops(mid)
    message = second_message(mid, relay)
    sum_mid = finish(mid, message, last_mid).astype(BF16)
    sum_mid, own[2], own[3] = tie((sum_mid, own[2], own[3]))

    pre_1, pre_3, back_1, back_3 = split_rows(sum_mid, 4)
    from_z = shift_between_pairs(jnp.concatenate([pre_3, back_3]), -2).astype(F32)
    from_z = from_z + shift_between_pairs(jnp.concatenate([pre_1, back_1]), 1).astype(F32)
    from_z = tie(from_z + shift_between_pairs(sum_far, 3).astype(F32))
    relay, last_own = first_hops(own)
    total = finish(own, second_message(own, relay), last_own)
    total = total + from_z
    total = total + swap_in_pair(total.astype(BF16)).astype(F32)
    pre_act, grad_hidden = total[:unit], total[unit:]
    hidden = gelu_tanh(pre_act).astype(BF16)
    grad_pre = (grad_hidden * gelu_slope(pre_act)).astype(BF16)

    def neighbours(message):
        return shift_apart(message, "y", -1), shift_apart(message, "y", 1)

    mine = jnp.concatenate([hidden, grad_pre])
    have_1 = shift_between_pairs(mine, 1)
    have_3 = swap_in_pair(have_1)
    have_2 = shift_between_pairs(have_1, -2)
    have_near = jnp.concatenate([mine, have_1])
    next_near, last_near = neighbours(have_near)
    next_near, have_2, have_3 = tie((next_near, have_2, have_3))
    relay_near = shift_apart(next_near, "y", -1)
    have_far = jnp.concatenate([have_3, have_2])
    next_far, last_far = neighbours(have_far)
    relay_near, relay_far = tie((relay_near, shift_apart(next_far, "y", -1)))

    stages = (
        (((0, 1), (3, 0, 1), (last_near, have_near, next_near)),),
        (
            ((0, 1), (2,), (relay_near,)),
            ((3, 2), (3, 0, 1), (last_far, have_far, next_far)),
            ((3, 2), (2,), (relay_far,)),
        ),
    )
    in_blocks, sums = {}, (0.0, 0.0)
    for stage in stages:
        hidden, grad_pre, rows = [], [], []
        for js, es, messages in stage:
            parts = [split_rows(message, 2 * len(js)) for message in messages]
            hidden += [row for p in parts for row in p[0::2]]
            grad_pre += [row for p in parts for row in p[1::2]]
            rows += [both[e, j] for e in es for j in js]
        hidden, grad_pre, rows = (jnp.concatenate(v) for v in (hidden, grad_pre, rows))
        in_part = iter(split_rows(contract(grad_pre, up_weight, 1, 1), rows.shape[0] // unit))
        for js, es, _ in stage:
            for _ in es:
                for j in js:
                    in_blocks.setdefault(j, []).append(next(in_part))
        sums = tie(sums)
        sums = (
            sums[0] + contract(rows[:, :width], grad_pre, 0, 0),
            sums[1] + contract(hidden, rows[:, width:], 0, 0),
        )
    up_sum, down_sum = sums

    in_total = jnp.stack([jnp.stack(in_blocks[j]) for j in range(n_pair)], axis=1)
    in_total = roll(in_total, 0, way * (x - y) + 1)
    in_total = roll(
        jnp.where(odd, in_total, in_total[:, ::-1]),
        1,
        jnp.where(odd, half * core - pair, half * core + n_pair - 1 - pair),
    )
    other = swap_cores(in_total[:, half:])
    in_chip = [in_total[e, :half] + other[-e % NX] for e in range(NX)]
    in_mine = in_chip[0] + shift(in_chip[2], "x", 2)
    in_mine = in_mine + shift_apart(in_chip[1], "x", 1) + shift_apart(in_chip[3], "x", -1)
    grad_in = in_mine.reshape(half * unit, width).astype(BF16)
    return grad_in, up_sum.astype(BF16), down_sum.astype(BF16)


def solution(mesh):
    grid = Mesh(mesh.devices.reshape(NZ, NY, NX, NCORE), ("z", "y", "x", "core"))
    return jax.shard_map(
        shards,
        mesh=grid,
        in_specs=(P(COL, ROW), P(COL, ROW), P(ROW, COL), P(COL, ROW)),
        out_specs=(P(COL, ROW), P(ROW, COL), P(COL, ROW)),
        check_vma=False,
    )
```

```python
import jax
import jax.numpy as jnp
from jax import lax
from jax.sharding import Mesh, PartitionSpec as P

F32, BF16 = jnp.float32, jnp.bfloat16
COL, ROW = ("x", "core"), ("z", "y")
NZ, NY, NX, NCORE = 8, 4, 4, 2
SIZES = {"z": NZ, "y": NY, "x": NX, "core": NCORE}


def contract(left, right, left_dim, right_dim):
    return lax.dot_general(
        left, right, (((left_dim,), (right_dim,)), ((), ())), preferred_element_type=F32
    )


def gelu_tanh(values):
    return jax.nn.gelu(values, approximate=True)


def gelu_slope(values):
    return jax.jvp(gelu_tanh, (values,), (jnp.ones_like(values),))[1]


def shift(value, axis, by):
    n = SIZES[axis]
    return lax.ppermute(value, axis, [(i, (i + by) % n) for i in range(n)])


def shift_apart(value, axis, by):
    n = SIZES[axis]
    pairs = [
        (i * NCORE + core, (i + by * (1 - 2 * core)) % n * NCORE + core)
        for i in range(n)
        for core in range(NCORE)
    ]
    return lax.ppermute(value, (axis, "core"), pairs)


def shift_between_pairs(value, by):
    return lax.ppermute(value, "z", [(i, (i + by * (2 * (i % 2) - 1)) % NZ) for i in range(NZ)])


def swap_in_pair(value):
    return lax.ppermute(value, "z", [(i, i ^ 1) for i in range(NZ)])


def swap_cores(value):
    return lax.ppermute(value, "core", [(0, 1), (1, 0)])


def tie(values):
    return lax.optimization_barrier(values)


def roll(value, axis, start):
    n = value.shape[axis]
    return lax.dynamic_slice_in_dim(
        jnp.concatenate([value, value], axis=axis), lax.rem(start + n, n), n, axis=axis
    )


def split_rows(value, n):
    rows = value.shape[0] // n
    return [value[i * rows : (i + 1) * rows] for i in range(n)]


def shards(tokens, grad_out, up_weight, down_weight):
    width = tokens.shape[1]
    z, y, x, core = (lax.axis_index(name) for name in ("z", "y", "x", "core"))
    way = 1 - 2 * core
    n_pair = NZ // 2
    half = n_pair // 2
    unit = tokens.shape[0] // half
    both = jnp.concatenate([tokens, grad_out], axis=1).reshape(half, unit, 2 * width)
    chip = jnp.concatenate([both, swap_cores(both)])
    next_x, far_x, last_x = (shift_apart(chip, "x", -1), shift(chip, "x", 2), shift_apart(chip, "x", 1))
    both = jnp.stack([chip, next_x, far_x, last_x])
    pair, odd = z // 2, z % 2 == 1
    both = roll(both, 0, way * (y - x))
    both = roll(
        jnp.where(odd, both, both[:, ::-1]),
        1,
        jnp.where(odd, pair - half * core, half * core + n_pair - 1 - pair),
    )

    order = (2, 1, 3, 0)
    rows = jnp.concatenate([both[:, j] for j in order], axis=1).reshape(-1, 2 * width)
    pre = split_rows(jnp.dot(rows[:, :width], up_weight, preferred_element_type=F32), NY)
    back = split_rows(contract(rows[:, width:], down_weight, 1, 1), NY)

    def parts_of(first, last):
        at = slice(first * unit, last * unit)
        parts = [jnp.concatenate([p[at], b[at]]) for p, b in zip(pre, back, strict=True)]
        return [parts[0], parts[1], parts[2].astype(BF16), parts[3].astype(BF16)]

    def first_hops(parts):
        return shift_apart(parts[2], "y", 1), shift_apart(parts[3], "y", -1)

    def second_message(parts, relay):
        return (parts[1] + relay.astype(F32)).astype(BF16)

    def finish(parts, message, last):
        return parts[0] + shift_apart(message, "y", 1).astype(F32) + last.astype(F32)

    far, mid, own = parts_of(0, 1), parts_of(1, 3), parts_of(3, 4)
    relay, last_far = first_hops(far)
    message = second_message(far, relay)
    sum_far = finish(far, message, last_far).astype(BF16)
    relay, last_mid = first_hops(mid)
    message = second_message(mid, relay)
    sum_mid = finish(mid, message, last_mid).astype(BF16)
    sum_mid, own[2], own[3] = tie((sum_mid, own[2], own[3]))

    pre_1, pre_3, back_1, back_3 = split_rows(sum_mid, 4)
    from_z = shift_between_pairs(jnp.concatenate([pre_3, back_3]), -2).astype(F32)
    from_z = from_z + shift_between_pairs(jnp.concatenate([pre_1, back_1]), 1).astype(F32)
    from_z = tie(from_z + shift_between_pairs(sum_far, 3).astype(F32))
    relay, last_own = first_hops(own)
    total = finish(own, second_message(own, relay), last_own)
    total = total + from_z
    total = total + swap_in_pair(total.astype(BF16)).astype(F32)
    pre_act, grad_hidden = total[:unit], total[unit:]
    hidden = gelu_tanh(pre_act).astype(BF16)
    grad_pre = (grad_hidden * gelu_slope(pre_act)).astype(BF16)

    def neighbours(message):
        return shift_apart(message, "y", -1), shift_apart(message, "y", 1)

    mine = jnp.concatenate([hidden, grad_pre])
    have_1 = shift_between_pairs(mine, 1)
    have_3 = swap_in_pair(have_1)
    have_2 = shift_between_pairs(have_1, -2)
    have_near = jnp.concatenate([mine, have_1])
    next_near, last_near = neighbours(have_near)
    relay_near = shift_apart(next_near, "y", -1)
    have_far = jnp.concatenate([have_3, have_2])
    next_far, last_far = neighbours(have_far)
    relay_near, relay_far = tie((relay_near, shift_apart(next_far, "y", -1)))

    stages = (
        (((0, 1), (3, 0, 1), (last_near, have_near, next_near)),),
        (
            ((0, 1), (2,), (relay_near,)),
            ((3, 2), (3, 0, 1), (last_far, have_far, next_far)),
            ((3, 2), (2,), (relay_far,)),
        ),
    )
    in_blocks, sums = {}, (0.0, 0.0)
    for stage in stages:
        hidden, grad_pre, rows = [], [], []
        for js, es, messages in stage:
            parts = [split_rows(message, 2 * len(js)) for message in messages]
            hidden += [row for p in parts for row in p[0::2]]
            grad_pre += [row for p in parts for row in p[1::2]]
            rows += [both[e, j] for e in es for j in js]
        hidden, grad_pre, rows = (jnp.concatenate(v) for v in (hidden, grad_pre, rows))
        in_part = iter(split_rows(contract(grad_pre, up_weight, 1, 1), rows.shape[0] // unit))
        for js, es, _ in stage:
            for _ in es:
                for j in js:
                    in_blocks.setdefault(j, []).append(next(in_part))
        sums = tie(sums)
        sums = (
            sums[0] + contract(rows[:, :width], grad_pre, 0, 0),
            sums[1] + contract(hidden, rows[:, width:], 0, 0),
        )
    up_sum, down_sum = sums

    in_total = jnp.stack([jnp.stack(in_blocks[j]) for j in range(n_pair)], axis=1)
    in_total = roll(in_total, 0, way * (x - y) + 1)
    in_total = roll(
        jnp.where(odd, in_total, in_total[:, ::-1]),
        1,
        jnp.where(odd, half * core - pair, half * core + n_pair - 1 - pair),
    )
    other = swap_cores(in_total[:, half:])
    in_chip = [in_total[e, :half] + other[-e % NX] for e in range(NX)]
    in_mine = in_chip[0] + shift(in_chip[2], "x", 2)
    in_mine = in_mine + shift_apart(in_chip[1], "x", 1) + shift_apart(in_chip[3], "x", -1)
    grad_in = in_mine.reshape(half * unit, width).astype(BF16)
    return grad_in, up_sum.astype(BF16), down_sum.astype(BF16)


def solution(mesh):
    grid = Mesh(mesh.devices.reshape(NZ, NY, NX, NCORE), ("z", "y", "x", "core"))
    return jax.shard_map(
        shards,
        mesh=grid,
        in_specs=(P(COL, ROW), P(COL, ROW), P(ROW, COL), P(COL, ROW)),
        out_specs=(P(COL, ROW), P(ROW, COL), P(COL, ROW)),
        check_vma=False,
    )
```

```python
import jax
import jax.numpy as jnp
from jax import lax
from jax.sharding import Mesh, PartitionSpec as P

F32, BF16 = jnp.float32, jnp.bfloat16
COL, ROW = ("x", "core"), ("z", "y")
NZ, NY, NX, NCORE = 8, 4, 4, 2
SIZES = {"z": NZ, "y": NY, "x": NX, "core": NCORE}


def contract(left, right, left_dim, right_dim):
    return lax.dot_general(
        left, right, (((left_dim,), (right_dim,)), ((), ())), preferred_element_type=F32
    )


def gelu_tanh(values):
    return jax.nn.gelu(values, approximate=True)


def gelu_slope(values):
    return jax.jvp(gelu_tanh, (values,), (jnp.ones_like(values),))[1]


def shift(value, axis, by):
    n = SIZES[axis]
    return lax.ppermute(value, axis, [(i, (i + by) % n) for i in range(n)])


def shift_apart(value, axis, by):
    n = SIZES[axis]
    pairs = [
        (i * NCORE + core, (i + by * (1 - 2 * core)) % n * NCORE + core)
        for i in range(n)
        for core in range(NCORE)
    ]
    return lax.ppermute(value, (axis, "core"), pairs)


def shift_between_pairs(value, by):
    return lax.ppermute(value, "z", [(i, (i + by * (2 * (i % 2) - 1)) % NZ) for i in range(NZ)])


def swap_in_pair(value):
    return lax.ppermute(value, "z", [(i, i ^ 1) for i in range(NZ)])


def swap_cores(value):
    return lax.ppermute(value, "core", [(0, 1), (1, 0)])


def tie(values):
    return lax.optimization_barrier(values)


def roll(value, axis, start):
    n = value.shape[axis]
    return lax.dynamic_slice_in_dim(
        jnp.concatenate([value, value], axis=axis), lax.rem(start + n, n), n, axis=axis
    )


def split_rows(value, n):
    rows = value.shape[0] // n
    return [value[i * rows : (i + 1) * rows] for i in range(n)]


def shards(tokens, grad_out, up_weight, down_weight):
    width = tokens.shape[1]
    z, y, x, core = (lax.axis_index(name) for name in ("z", "y", "x", "core"))
    way = 1 - 2 * core
    n_pair = NZ // 2
    half = n_pair // 2
    unit = tokens.shape[0] // half
    both = jnp.concatenate([tokens, grad_out], axis=1).reshape(half, unit, 2 * width)
    chip = jnp.concatenate([both, swap_cores(both)])
    next_x, far_x, last_x = (shift_apart(chip, "x", -1), shift(chip, "x", 2), shift_apart(chip, "x", 1))
    both = jnp.stack([chip, next_x, far_x, last_x])
    pair, odd = z // 2, z % 2 == 1
    both = roll(both, 0, way * (y - x))
    both = roll(
        jnp.where(odd, both, both[:, ::-1]),
        1,
        jnp.where(odd, pair - half * core, half * core + n_pair - 1 - pair),
    )

    order = (2, 1, 3, 0)
    rows = jnp.concatenate([both[:, j] for j in order], axis=1).reshape(-1, 2 * width)
    pre = split_rows(jnp.dot(rows[:, :width], up_weight, preferred_element_type=F32), NY)
    back = split_rows(contract(rows[:, width:], down_weight, 1, 1), NY)

    def parts_of(first, last):
        at = slice(first * unit, last * unit)
        parts = [jnp.concatenate([p[at], b[at]]) for p, b in zip(pre, back, strict=True)]
        return [parts[0], parts[1], parts[2].astype(BF16), parts[3].astype(BF16)]

    def first_hops(parts):
        return shift_apart(parts[2], "y", 1), shift_apart(parts[3], "y", -1)

    def second_message(parts, relay):
        return (parts[1] + relay.astype(F32)).astype(BF16)

    def finish(parts, message, last):
        return parts[0] + shift_apart(message, "y", 1).astype(F32) + last.astype(F32)

    far, mid, own = parts_of(0, 1), parts_of(1, 3), parts_of(3, 4)
    relay, last_far = first_hops(far)
    message = second_message(far, relay)
    sum_far = finish(far, message, last_far).astype(BF16)
    relay, last_mid = first_hops(mid)
    message = second_message(mid, relay)
    sum_mid = finish(mid, message, last_mid).astype(BF16)
    sum_mid, own[2] = tie((sum_mid, own[2]))

    pre_1, pre_3, back_1, back_3 = split_rows(sum_mid, 4)
    from_z = shift_between_pairs(jnp.concatenate([pre_3, back_3]), -2).astype(F32)
    from_z = from_z + shift_between_pairs(jnp.concatenate([pre_1, back_1]), 1).astype(F32)
    from_z = tie(from_z + shift_between_pairs(sum_far, 3).astype(F32))
    relay = shift_apart(own[2], "y", 1)
    message, own[3] = tie((second_message(own, relay), own[3]))
    total = finish(own, message, shift_apart(own[3], "y", -1))
    total = total + from_z
    total = total + swap_in_pair(total.astype(BF16)).astype(F32)
    pre_act, grad_hidden = total[:unit], total[unit:]
    hidden = gelu_tanh(pre_act).astype(BF16)
    grad_pre = (grad_hidden * gelu_slope(pre_act)).astype(BF16)

    def neighbours(message):
        return shift_apart(message, "y", -1), shift_apart(message, "y", 1)

    mine = jnp.concatenate([hidden, grad_pre])
    have_1 = shift_between_pairs(mine, 1)
    have_3 = swap_in_pair(have_1)
    have_2 = shift_between_pairs(have_1, -2)
    have_near = jnp.concatenate([mine, have_1])
    next_near, last_near = neighbours(have_near)
    relay_near = shift_apart(next_near, "y", -1)
    have_far = jnp.concatenate([have_3, have_2])
    next_far, last_far = neighbours(have_far)
    relay_near, relay_far = tie((relay_near, shift_apart(next_far, "y", -1)))

    stages = (
        (((0, 1), (3, 0, 1), (last_near, have_near, next_near)),),
        (
            ((0, 1), (2,), (relay_near,)),
            ((3, 2), (3, 0, 1), (last_far, have_far, next_far)),
            ((3, 2), (2,), (relay_far,)),
        ),
    )
    in_blocks, sums = {}, (0.0, 0.0)
    for stage in stages:
        hidden, grad_pre, rows = [], [], []
        for js, es, messages in stage:
            parts = [split_rows(message, 2 * len(js)) for message in messages]
            hidden += [row for p in parts for row in p[0::2]]
            grad_pre += [row for p in parts for row in p[1::2]]
            rows += [both[e, j] for e in es for j in js]
        hidden, grad_pre, rows = (jnp.concatenate(v) for v in (hidden, grad_pre, rows))
        in_part = iter(split_rows(contract(grad_pre, up_weight, 1, 1), rows.shape[0] // unit))
        for js, es, _ in stage:
            for _ in es:
                for j in js:
                    in_blocks.setdefault(j, []).append(next(in_part))
        sums = tie(sums)
        sums = (
            sums[0] + contract(rows[:, :width], grad_pre, 0, 0),
            sums[1] + contract(hidden, rows[:, width:], 0, 0),
        )
    up_sum, down_sum = sums

    in_total = jnp.stack([jnp.stack(in_blocks[j]) for j in range(n_pair)], axis=1)
    in_total = roll(in_total, 0, way * (x - y) + 1)
    in_total = roll(
        jnp.where(odd, in_total, in_total[:, ::-1]),
        1,
        jnp.where(odd, half * core - pair, half * core + n_pair - 1 - pair),
    )
    other = swap_cores(in_total[:, half:])
    in_chip = [in_total[e, :half] + other[-e % NX] for e in range(NX)]
    in_mine = in_chip[0] + shift(in_chip[2], "x", 2)
    in_mine = in_mine + shift_apart(in_chip[1], "x", 1) + shift_apart(in_chip[3], "x", -1)
    grad_in = in_mine.reshape(half * unit, width).astype(BF16)
    return grad_in, up_sum.astype(BF16), down_sum.astype(BF16)


def solution(mesh):
    grid = Mesh(mesh.devices.reshape(NZ, NY, NX, NCORE), ("z", "y", "x", "core"))
    return jax.shard_map(
        shards,
        mesh=grid,
        in_specs=(P(COL, ROW), P(COL, ROW), P(ROW, COL), P(COL, ROW)),
        out_specs=(P(COL, ROW), P(ROW, COL), P(COL, ROW)),
        check_vma=False,
    )
```
